256 devices in a mesh: tm: 8 (over y, z_hi), height: 4 (over z_lo), tensor: 8 (over x, core).
Axes of the slice: x: 4, y: 4, z: 8 (z_hi: 2, z_lo: 4; z = z_hi * 4 + z_lo), core: 2. Of those that a mesh axis runs over, the one named last changes fastest.
Arguments:
- query: bfloat16 [8, 4, 1, 384, 3072], P('tm', 'height', None, 'tensor'), may hold values from -200 to 200
- keys: bfloat16 [8, 4, 1, 384, 3072], P('tm', 'height', None, 'tensor'), may hold values from -7 to 7
- values: bfloat16 [8, 4, 1, 384, 3072], P('tm', 'height', None, 'tensor'), may hold values from -6 to 6
- cotangent: bfloat16 [8, 4, 1, 384, 3072], P('tm', 'height', None, 'tensor'), may hold values from -6 to 6
- extents: int32 [8, 4, 1, 3], replicated, may hold values from 0 to 1, as said below
Outputs:
- attended: bfloat16 [8, 4, 1, 384, 3072], P('tm', 'height', None, 'tensor')
- query_grad: bfloat16 [8, 4, 1, 384, 3072], P('tm', 'height', None, 'tensor')
- key_grad: bfloat16 [8, 4, 1, 384, 3072], P('tm', 'height', None, 'tensor')
- value_grad: bfloat16 [8, 4, 1, 384, 3072], P('tm', 'height', None, 'tensor')
The draws below stay inside these ranges and needn't reach their ends.
Inputs may be any that keep to these rules, and one draw needn't show every extreme that they name: `extents`: window half-widths in tiles; the half-width along frames is 1 on every tile, the half-width along rows is 1 on every tile of an even frame index.
All inputs are finite; a program needn't handle non-finite values.
Results may differ from the reference program's by a relative error of at most 0.019.
Values may be sent and summed in bfloat16 or wider, within the bound.
A program may use at most 128 MiB of HBM per device.

```python
import math
import jax
import jax.numpy as jnp
import numpy as np
from jax import lax

HEADS = 24
HD = 128
D = 3072
TILE = 384
TILES_W = 1
TILES_T = 8
TILES_H = 4


def shared_keys(key):
    return jnp.clip(jax.random.normal(key, (TILES_T, TILES_H, TILES_W, TILE, D), jnp.float32), -6.0, 6.0)


def draw_keys(key, part):
    base = shared_keys(key)
    return base.astype(jnp.bfloat16)


def draw_query(key, part):
    key = jax.random.fold_in(key, 5)
    fresh = jnp.clip(jax.random.normal(key, (TILES_T, TILES_H, TILES_W, TILE, D), jnp.float32), -6.0, 6.0)
    return fresh.astype(jnp.bfloat16)


def draw_extents(key, part):
    key = jax.random.fold_in(key, 13)
    drawn = jax.random.randint(key, (TILES_T, TILES_H, TILES_W, 3), 0, 2, jnp.int32)
    frame_index = jnp.arange(TILES_T, dtype=jnp.int32)[:, None, None]
    even_frame = frame_index % 2 == 0
    rows_part = jnp.where(even_frame, jnp.int32(1), drawn[..., 1])
    rows_part = rows_part.at[1, 0, 0].set(jnp.int32(0))
    frames_part = jnp.ones_like(drawn[..., 0])
    return jnp.stack((frames_part, rows_part, drawn[..., 2]), axis=-1).astype(jnp.int32)


def level_of(key, dims, shards, low, high):
    loudness, own = 1.0, jax.random.fold_in(key, 6)
    for dim, blocks in shards:
        heights = jnp.exp(jax.random.uniform(jax.random.fold_in(own, dim), (blocks,), jnp.float32, low / len(shards), high / len(shards)))
        loudness = loudness * jnp.repeat(heights, dims[dim] // blocks).reshape([-1 if axis == dim else 1 for axis in range(len(dims))])
    return loudness


def normal_values(own_key, dims, spread, reach, shards=(), kind=jnp.bfloat16):
    result = jax.random.normal(own_key, dims, jnp.float32) * spread
    if len(shards) > 0:
        result = level_of(own_key, dims, shards, -0.22, 0.18) * result
    return jnp.clip(result, min=-reach, max=reach).astype(kind)


def setup_inputs(seed: int = 0) -> dict:
    key_of = jax.random.split(jax.random.key(seed), 6)
    return {
        "query": draw_query(jax.random.fold_in(key_of[5], 71), 0),
        "keys": draw_keys(jax.random.fold_in(key_of[5], 71), 0),
        "values": normal_values(key_of[2], (TILES_T, TILES_H, TILES_W, TILE, D), 1.0, 6.0, ((0, 8), (1, 4), (3, 8))),
        "cotangent": normal_values(key_of[3], (TILES_T, TILES_H, TILES_W, TILE, D), 1.0, 6.0, ((0, 8), (1, 4), (3, 8))),
        "extents": draw_extents(jax.random.fold_in(key_of[5], 71), 0),
    }


def offset_table(reach_w):
    listed = [(a, b, c) for a in (-1, 0, 1) for b in (-1, 0, 1) for c in range(-reach_w, reach_w + 1)]
    return np.array(listed, dtype=np.int32)

def to_float(array):
    return array.astype(jnp.float32)

def attend(query_rows, every_key_row, every_value_row, output_gradient, allowed, score_scale):
    scores = jnp.einsum('aqhd,bkhd->haqbk', to_float(query_rows), to_float(every_key_row)) * score_scale
    allowed_rows = allowed[None, :, None, :, None]
    row_max = lax.optimization_barrier(jnp.max(jnp.where(allowed_rows, scores, -jnp.inf), axis=(3, 4)))
    raw_weights = jnp.where(allowed_rows, jnp.exp(scores - row_max[..., None, None]), 0.0)
    row_sum = lax.optimization_barrier(jnp.sum(raw_weights, axis=(3, 4)))
    prob = raw_weights / row_sum[..., None, None]
    softmax_weight = lax.optimization_barrier(prob.astype(jnp.bfloat16))
    attended = jnp.einsum('haqbk,bkhd->aqhd', to_float(softmax_weight), to_float(every_value_row)).astype(jnp.bfloat16)
    row_dot = jnp.transpose(lax.optimization_barrier(jnp.sum(to_float(output_gradient) * to_float(attended), axis=-1)), (2, 0, 1))
    probability_gradient = jnp.einsum('aqhd,bkhd->haqbk', to_float(output_gradient), to_float(every_value_row))
    logit_gradient = lax.optimization_barrier((prob * (probability_gradient - row_dot[..., None, None])).astype(jnp.bfloat16))
    query_grad = (jnp.einsum('haqbk,bkhd->aqhd', to_float(logit_gradient), to_float(every_key_row)) * score_scale).astype(jnp.bfloat16)
    return (attended, query_grad, jnp.stack((row_max, row_sum, row_dot)))

def key_side(query_rows, output_gradient, row_stats, keys_own, values_own, allowed, score_scale):
    scores = jnp.einsum('aqhd,bkhd->haqbk', to_float(query_rows), to_float(keys_own)) * score_scale
    allowed_rows = allowed[None, :, None, :, None]
    row_max = row_stats[0][..., None, None]
    row_sum = jnp.maximum(row_stats[1], 1.0)[..., None, None]
    row_dot = row_stats[2][..., None, None]
    prob = jnp.where(allowed_rows, jnp.exp(scores - row_max) / row_sum, 0.0)
    softmax_weight = lax.optimization_barrier(prob.astype(jnp.bfloat16))
    probability_gradient = jnp.einsum('aqhd,bkhd->haqbk', to_float(output_gradient), to_float(values_own))
    logit_gradient = lax.optimization_barrier((prob * (probability_gradient - row_dot)).astype(jnp.bfloat16))
    key_grad = (jnp.einsum('haqbk,aqhd->bkhd', to_float(logit_gradient), to_float(query_rows)) * score_scale).astype(jnp.bfloat16)
    value_grad = jnp.einsum('haqbk,aqhd->bkhd', to_float(softmax_weight), to_float(output_gradient)).astype(jnp.bfloat16)
    return (key_grad, value_grad)

def reference(query, keys, values, cotangent, extents):
    score_scale = 1.0 / math.sqrt(HD)
    reach_w = min(1, TILES_W - 1)
    span_w = 2 * reach_w + 1
    table = jnp.asarray(offset_table(reach_w))
    limits = jnp.array([TILES_T, TILES_H, TILES_W], dtype=jnp.int32)
    pad_five = ((1, 1), (1, 1), (reach_w, reach_w), (0, 0), (0, 0))
    query_pad = jnp.pad(query, pad_five)
    keys_pad = jnp.pad(keys, pad_five)
    values_pad = jnp.pad(values, pad_five)
    grads_pad = jnp.pad(cotangent, pad_five)
    spans_pad = jnp.pad(extents, ((1, 1), (1, 1), (reach_w, reach_w), (0, 0)))
    grid_t, grid_h, grid_w = jnp.meshgrid(jnp.arange(TILES_T), jnp.arange(TILES_H), jnp.arange(TILES_W), indexing='ij')
    tile_list = jnp.stack([grid_t.ravel(), grid_h.ravel(), grid_w.ravel()], axis=1).astype(jnp.int32)

    def region(array, tile_index):
        start = [tile_index[0], tile_index[1], tile_index[2]] + [jnp.int32(0)] * (array.ndim - 3)
        sizes = (3, 3, span_w) + array.shape[3:]
        return lax.dynamic_slice(array, start, sizes).reshape((-1,) + array.shape[3:])

    def single(array, tile_index):
        start = [tile_index[0], tile_index[1], tile_index[2]] + [jnp.int32(0)] * (array.ndim - 3)
        sizes = (1, 1, 1) + array.shape[3:]
        return lax.dynamic_slice(array, start, sizes).reshape((-1,) + array.shape[3:])

    def by_heads(array):
        return array.reshape(array.shape[0], TILE, HEADS, HD)

    def first_pass(tile_index):
        nearby = tile_index[None, :] + table
        inside = jnp.all((nearby >= 0) & (nearby < limits[None, :]), axis=1)
        window = extents[tile_index[0], tile_index[1], tile_index[2]]
        allowed = (jnp.all(jnp.abs(table) <= window[None, :], axis=1) & inside)[None, :]
        attended, query_grad, row_stats = attend(by_heads(single(query, tile_index)), by_heads(region(keys_pad, tile_index)), by_heads(region(values_pad, tile_index)), by_heads(single(cotangent, tile_index)), allowed, score_scale)
        return (attended.reshape(TILE, D), query_grad.reshape(TILE, D), row_stats[:, :, 0, :])
    attended, query_grad, row_stats = lax.map(first_pass, tile_list)
    grid_shape = (TILES_T, TILES_H, TILES_W)
    stats_grid = row_stats.reshape(grid_shape + (3, HEADS, TILE))
    stats_pad = jnp.pad(stats_grid, ((1, 1), (1, 1), (reach_w, reach_w), (0, 0), (0, 0), (0, 0)))

    def second_pass(tile_index):
        nearby = tile_index[None, :] + table
        inside = jnp.all((nearby >= 0) & (nearby < limits[None, :]), axis=1)
        windows = region(spans_pad, tile_index)
        allowed = (jnp.all(jnp.abs(table) <= windows, axis=1) & inside)[:, None]
        near_stats = jnp.transpose(region(stats_pad, tile_index), (1, 2, 0, 3))
        key_grad, value_grad = key_side(by_heads(region(query_pad, tile_index)), by_heads(region(grads_pad, tile_index)), near_stats, by_heads(single(keys, tile_index)), by_heads(single(values, tile_index)), allowed, score_scale)
        return (key_grad.reshape(TILE, D), value_grad.reshape(TILE, D))
    key_grad, value_grad = lax.map(second_pass, tile_list)
    full_shape = grid_shape + (TILE, D)
    return (attended.reshape(full_shape), query_grad.reshape(full_shape), key_grad.reshape(full_shape), value_grad.reshape(full_shape))
```

```python
import functools
import math

import jax
import jax.numpy as jnp
from jax import lax
from jax.experimental import pallas as pl
from jax.experimental.pallas import tpu as pltpu
from jax.sharding import PartitionSpec as P

MESH = pl.DeviceIdType.MESH
HD = 128
ROWS = 4
FRAMES = 8
NEG = -1e30
BF = jnp.bfloat16
F32 = jnp.float32


def dot(a, b):
    return jnp.dot(a, b, preferred_element_type=F32)


def head_of(x, z):
    low = z % 4
    return 6 * x + 3 * (z // 4) + low - (low > x).astype(jnp.int32)


def place(y, z, x, core):
    return (2 * y + z // 4, z % 4, 2 * x + core)


def kernel(
    tile, chunk,
    ext_ref, q_ref, k_ref, v_ref, g_ref,
    o_att, o_dq, o_dk, o_dv,
    qb, gb, kb, vb, kt, vt, qt, s_all, e_all,
    att_s, dq_s, dk_s, dv_s, dk_acc, dv_acc, dk_ret, dv_ret, dk_got, dv_got,
    in_send, in_recv, halo_send, halo_recv, ret_send, ret_recv, out_send, out_recv,
):
    scale = 1.0 / math.sqrt(HD)
    c2 = scale * math.log2(math.e)
    tm, zlo, ten = (lax.axis_index(a) for a in ("tm", "height", "tensor"))
    y, zhi, x, core = tm // 2, tm % 2, ten // 2, ten % 2
    z = zhi * 4 + zlo
    worker = zlo != x
    frame = 2 * y + core
    mine = worker & (core == zhi)
    has_prev, has_next = frame > 0, frame < FRAMES - 1
    prev_dev = place((frame - 1 + FRAMES) % FRAMES // 2, z, x, 1 - core)
    next_dev = place((frame + 1) % FRAMES // 2, z, x, 1 - core)
    head = head_of(x, z)

    def rows(h):
        return pl.ds(h * tile, tile)

    def source(i):
        return (frame, i // 8, i % 8)

    barrier = pltpu.get_barrier_semaphore()

    def greet(dev):
        pl.semaphore_signal(barrier, inc=1, device_id=dev, device_id_type=MESH)

    @pl.when(worker)
    def _():
        @pl.loop(0, 32)
        def _(i):
            me = (core == zhi) & (i // 8 == zlo) & (i % 8 == ten)

            @pl.when(jnp.logical_not(me))
            def _():
                greet(source(i))

        @pl.when(has_prev)
        def _():
            greet(prev_dev)

        @pl.when(has_next)
        def _():
            greet(next_dev)

    near = has_prev.astype(jnp.int32) + has_next.astype(jnp.int32)
    pl.semaphore_wait(barrier, 24 - mine.astype(jnp.int32) + near * worker.astype(jnp.int32))

    arrays = ((k_ref, kb, 4), (v_ref, vb, 4), (q_ref, qb, 0), (g_ref, gb, 0))

    def put(h):
        return pl.ds(pl.multiple_of(h * tile + ten * chunk, 16), chunk)

    for a, (src, buf, first) in enumerate(arrays):
        @pl.loop(0, 32)
        def _(i, a=a, src=src, buf=buf, first=first):
            x2, z2 = (x + i // 8) % 4, (z + i % 8) % 8
            block = src.at[:, pl.ds(pl.multiple_of(head_of(x2, z2) * HD, HD), HD)]
            dst = buf.at[put(first + zlo)]
            sem = in_recv.at[a, zlo]
            me = (i == 0) & (core == zhi)

            @pl.when((z2 % 4 != x2) & me)
            def _():
                pltpu.make_async_copy(block, dst, sem).start()

            @pl.when((z2 % 4 != x2) & jnp.logical_not(me))
            def _():
                pltpu.make_async_remote_copy(
                    block, dst, in_send.at[a], sem, device_id=place(y, z2, x2, zhi), device_id_type=MESH
                ).start()

    def wait_bytes(ref, sem):
        pltpu.make_async_copy(ref, ref, sem).wait()

    def halo(src, dst, send, recv, dev):
        return pltpu.make_async_remote_copy(src, dst, send, recv, device_id=dev, device_id_type=MESH)

    outs = ((att_s, o_att), (dq_s, o_dq), (dk_s, o_dk), (dv_s, o_dv))

    def send_out(a, h):
        stage, out = outs[a]
        cols = pl.ds(pl.multiple_of(head * HD, HD), HD)

        @pl.loop(0, 8)
        def _(i):
            src = stage.at[pl.ds(pl.multiple_of(h * tile + i * chunk, 16), chunk)]
            dst = out.at[:, cols]
            me = (core == zhi) & (zlo == h) & (i == ten)

            @pl.when(me)
            def _():
                pltpu.make_async_copy(src, dst, out_recv.at[a]).start()

            @pl.when(jnp.logical_not(me))
            def _():
                pltpu.make_async_remote_copy(
                    src, dst, out_send.at[a], out_recv.at[a], device_id=(frame, h, i), device_id_type=MESH
                ).start()

    sides = ((0, has_prev, prev_dev), (1, has_next, next_dev))

    def key_frames(h0, n, fn):
        pass

    @pl.when(worker)
    def _():
        for side, has, dev in sides:
            @pl.when(jnp.logical_not(has))
            def _(side=side):
                here = pl.ds(side * 8 * tile, 4 * tile)
                for ref in (kb, vb):
                    ref[here, :] = jnp.zeros((4 * tile, HD), BF)

        for h in range(ROWS):
            for a, buf in enumerate((kb, vb)):
                wait_bytes(buf.at[rows(4 + h)], in_recv.at[a, h])
                for side, has, dev in sides:
                    @pl.when(has)
                    def _(side=side, dev=dev, a=a, buf=buf, h=h):
                        there = 2 - 2 * side
                        halo(
                            buf.at[rows(4 + h)], buf.at[rows(4 * there + h)],
                            halo_send.at[side, a], halo_recv.at[1 - side, a, h], dev,
                        ).start()

        dk_acc[...] = jnp.zeros_like(dk_acc)
        dv_acc[...] = jnp.zeros_like(dv_acc)

        def turn(f, h):
            r = rows(4 * f + h)
            kt[:, r] = kb[r, :].T
            vt[:, r] = vb[r, :].T

        for h in range(ROWS):
            turn(1, h)
        for h in range(ROWS):
            for side, has, dev in sides:
                @pl.when(has)
                def _(side=side, h=h):
                    for a, buf in enumerate((kb, vb)):
                        wait_bytes(buf.at[rows(8 * side + h)], halo_recv.at[side, a, h])
                turn(2 * side, h)

        for h in range(ROWS):
            lo, hi = max(h - 1, 0), min(h + 1, ROWS - 1)
            count = hi - lo + 1
            reach_t, reach_h = ext_ref[(frame * ROWS + h) * 3], ext_ref[(frame * ROWS + h) * 3 + 1]

            def where_is(j, lo=lo, count=count):
                f, r = j // count, lo + j % count
                return f, r, pl.ds(pl.multiple_of((4 * f + r) * tile, tile), tile)

            wait_bytes(qb.at[rows(h)], in_recv.at[2, h])
            qt[...] = qb[rows(h), :].T

            def scores(j, top, h=h, where_is=where_is, reach_t=reach_t, reach_h=reach_h):
                f, r, at = where_is(j)
                seen = (jnp.abs(f - 1) <= reach_t) & (jnp.abs(r - h) <= reach_h)
                seen &= (f + frame >= 1) & (f + frame <= FRAMES)
                s = dot(kb[at, :], qt[...])
                s = jnp.where(seen, s, NEG)
                s_all[pl.ds(pl.multiple_of(j * tile, tile), tile), :] = s
                return jnp.maximum(top, jnp.max(s.reshape(tile // 8, 8, tile), axis=0))

            top = lax.fori_loop(0, 3 * count, scores, jnp.full((8, tile), NEG, F32))
            top = jnp.max(top, axis=0, keepdims=True)

            def weigh(j, carry, where_is=where_is, top=top):
                total, acc = carry
                f, r, at = where_is(j)
                here = pl.ds(pl.multiple_of(j * tile, tile), tile)
                e = jnp.exp2((s_all[here, :] - top) * c2)
                eb = e.astype(BF)
                e_all[here, :] = eb
                total = total + jnp.sum(e.reshape(tile // 8, 8, tile), axis=0)
                return total, acc + dot(vt[:, at], eb)

            total, acc = lax.fori_loop(
                0, 3 * count, weigh, (jnp.zeros((8, tile), F32), jnp.zeros((HD, tile), F32))
            )
            inverse = 1.0 / jnp.sum(total, axis=0, keepdims=True)
            att = (acc * inverse).astype(BF)
            att_s[rows(h), :] = att.T
            wait_bytes(gb.at[rows(h)], in_recv.at[3, h])
            gt = (gb[rows(h), :].T.astype(F32) * inverse).astype(BF)
            gn = gt.T
            rd = jnp.sum(gt.astype(F32) * att.astype(F32), axis=0, keepdims=True)
            send_out(0, h)
            q = qb[rows(h), :]

            def back(j, acc, where_is=where_is, gt=gt, gn=gn, rd=rd, q=q):
                f, r, at = where_is(j)
                here = pl.ds(pl.multiple_of(j * tile, tile), tile)
                eb = e_all[here, :]
                dp = dot(vb[at, :], gt)
                ds = (eb.astype(F32) * (dp - rd)).astype(BF)
                dv_acc[at, :] += dot(eb, gn)
                dk_acc[at, :] += dot(ds, q)
                return acc + dot(kt[:, at], ds)

            dq = lax.fori_loop(0, 3 * count, back, jnp.zeros((HD, tile), F32))
            dq_s[rows(h), :] = (dq * scale).astype(BF).T
            send_out(1, h)

            done = [h - 1] if h < ROWS - 1 else [h - 1, h]
            for r in [r for r in done if r >= 0]:
                for side, has, dev in sides:
                    @pl.when(has)
                    def _(side=side, dev=dev, r=r):
                        for a, (acc_ref, ret, got, mult) in enumerate(
                            ((dk_acc, dk_ret, dk_got, scale), (dv_acc, dv_ret, dv_got, 1.0))
                        ):
                            ret[rows(4 * side + r), :] = (acc_ref[rows(8 * side + r), :] * mult).astype(BF)
                            halo(
                                ret.at[rows(4 * side + r)], got.at[rows(4 * (1 - side) + r)],
                                ret_send.at[side, a], ret_recv.at[1 - side, a, r], dev,
                            ).start()

        for r in range(ROWS):
            for a, (acc_ref, got, stage, mult) in enumerate(
                ((dk_acc, dk_got, dk_s, scale), (dv_acc, dv_got, dv_s, 1.0))
            ):
                for side, has, dev in sides:
                    @pl.when(has)
                    def _(side=side, a=a, r=r, got=got, acc_ref=acc_ref):
                        there = got.at[rows(4 * side + r)]
                        wait_bytes(there, ret_recv.at[side, a, r])
                        acc_ref[rows(4 + r), :] += there[...].astype(F32) * (1.0 / mult)
                stage[rows(r), :] = (acc_ref[rows(4 + r), :] * mult).astype(BF)
                send_out(2 + a, r)

        for side, has, dev in sides:
            @pl.when(has)
            def _(side=side):
                for a in range(2):
                    wait_bytes(kb.at[pl.ds(0, 4 * tile)], halo_send.at[side, a])
                    wait_bytes(dk_ret.at[pl.ds(0, 4 * tile)], ret_send.at[side, a])

        for a in range(4):
            @pl.when(core == zhi)
            def _(a=a):
                wait_bytes(att_s.at[pl.ds(0, 31 * chunk)], out_send.at[a])

            @pl.when(core != zhi)
            def _(a=a):
                wait_bytes(att_s, out_send.at[a])

    for a in range(4):
        @pl.when(mine)
        def _(a=a):
            wait_bytes(q_ref.at[:, pl.ds(0, 23 * HD)], in_send.at[a])

        @pl.when(jnp.logical_not(mine))
        def _(a=a):
            wait_bytes(q_ref, in_send.at[a])

    for a, (_, out) in enumerate(outs):
        wait_bytes(out, out_recv.at[a])


def solution(mesh):
    spec = P("tm", "height", None, "tensor", None)

    def shards(query, keys, values, cotangent, extents):
        shape = query.shape
        chunk, width = shape[3], shape[4]
        tile = chunk * mesh.shape["tensor"]
        flat = [a.reshape(chunk, width) for a in (query, keys, values, cotangent)]
        any_spec = pl.BlockSpec(memory_space=pl.ANY)
        frame_rows = ROWS * tile
        dma = pltpu.SemaphoreType.DMA
        outs = pl.pallas_call(
            functools.partial(kernel, tile, chunk),
            out_shape=[jax.ShapeDtypeStruct((chunk, width), BF)] * 4,
            in_specs=[pl.BlockSpec(memory_space=pltpu.SMEM)] + [any_spec] * 4,
            out_specs=[any_spec] * 4,
            scratch_shapes=[
                pltpu.VMEM((frame_rows, HD), BF),
                pltpu.VMEM((frame_rows, HD), BF),
                pltpu.VMEM((3 * frame_rows, HD), BF),
                pltpu.VMEM((3 * frame_rows, HD), BF),
                pltpu.VMEM((HD, 3 * frame_rows), BF),
                pltpu.VMEM((HD, 3 * frame_rows), BF),
                pltpu.VMEM((HD, tile), BF),
                pltpu.VMEM((9 * tile, tile), F32),
                pltpu.VMEM((9 * tile, tile), BF),
                *[pltpu.VMEM((frame_rows, HD), BF)] * 4,
                *[pltpu.VMEM((3 * frame_rows, HD), F32)] * 2,
                *[pltpu.VMEM((2 * frame_rows, HD), BF)] * 4,
                dma((4,)), dma((4, 4)), dma((2, 2)), dma((2, 2, 4)),
                dma((2, 2)), dma((2, 2, 4)), dma((4,)), dma((4,)),
            ],
            compiler_params=pltpu.CompilerParams(
                collective_id=0, has_side_effects=True, vmem_limit_bytes=56 * 2**20
            ),
            name="attention",
        )(extents.reshape(-1), *flat)
        return tuple(o.reshape(shape) for o in outs)

    return jax.shard_map(
        shards, mesh=mesh, in_specs=(spec, spec, spec, spec, P()), out_specs=(spec,) * 4, check_vma=False
    )
```

```python
import functools
import math

import jax
import jax.numpy as jnp
from jax import lax
from jax.experimental import pallas as pl
from jax.experimental.pallas import tpu as pltpu
from jax.sharding import PartitionSpec as P

MESH = pl.DeviceIdType.MESH
HD = 128
ROWS = 4
FRAMES = 8
LOW = -1e30
HIGH = 1e30
BF = jnp.bfloat16
F32 = jnp.float32


def dot(a, b):
    return jnp.dot(a, b, preferred_element_type=F32)


def head_of(x, z):
    low = z % 4
    return 6 * x + 3 * (z // 4) + low - (low > x).astype(jnp.int32)


def place(y, z, x, core):
    return (2 * y + z // 4, z % 4, 2 * x + core)


def kernel(
    tile, chunk,
    ext_ref, q_ref, k_ref, v_ref, g_ref,
    o_att, o_dq, o_dk, o_dv,
    qb, gb, kb, vb, kt, vt, qt, gt, gn, s_all, e_all, ds_all,
    att_s, dq_s, dk_s, dv_s, dv_own, dk_ret, dv_ret, dk_got, dv_got,
    in_send, in_recv, halo_send, halo_recv, ret_send, ret_recv, out_send, out_recv,
):
    scale = 1.0 / math.sqrt(HD)
    c2 = scale * math.log2(math.e)
    tm, zlo, ten = (lax.axis_index(a) for a in ("tm", "height", "tensor"))
    y, zhi, x, core = tm // 2, tm % 2, ten // 2, ten % 2
    z = zhi * 4 + zlo
    worker = zlo != x
    frame = 2 * y + core
    mine = worker & (core == zhi)
    has_prev, has_next = frame > 0, frame < FRAMES - 1
    prev_dev = place((frame - 1 + FRAMES) % FRAMES // 2, z, x, 1 - core)
    next_dev = place((frame + 1) % FRAMES // 2, z, x, 1 - core)
    sides = ((0, has_prev, prev_dev), (1, has_next, next_dev))
    head = head_of(x, z)

    def rows(first, count=1):
        return pl.ds(first * tile, count * tile)

    def source(i):
        return (frame, i // 8, i % 8)

    barrier = pltpu.get_barrier_semaphore()

    def greet(dev):
        pl.semaphore_signal(barrier, inc=1, device_id=dev, device_id_type=MESH)

    @pl.when(worker)
    def _():
        @pl.loop(0, 32)
        def _(i):
            me = (core == zhi) & (i // 8 == zlo) & (i % 8 == ten)

            @pl.when(jnp.logical_not(me))
            def _():
                greet(source(i))

        for _, has, dev in sides:
            @pl.when(has)
            def _(dev=dev):
                greet(dev)

    near = has_prev.astype(jnp.int32) + has_next.astype(jnp.int32)
    pl.semaphore_wait(barrier, 24 - mine.astype(jnp.int32) + near * worker.astype(jnp.int32))

    K, Q, V, G = range(4)
    arrays = ((k_ref, kb, 4), (q_ref, qb, 0), (v_ref, vb, 4), (g_ref, gb, 0))

    def put(first):
        return pl.ds(pl.multiple_of(first * tile + ten * chunk, 16), chunk)

    for a, (src, buf, first) in enumerate(arrays):
        @pl.loop(0, 32)
        def _(i, a=a, src=src, buf=buf, first=first):
            x2, z2 = (x + i // 8) % 4, (z + i % 8) % 8
            block = src.at[:, pl.ds(pl.multiple_of(head_of(x2, z2) * HD, HD), HD)]
            dst = buf.at[put(first + zlo)]
            sem = in_recv.at[a, zlo]
            me = (i == 0) & (core == zhi)

            @pl.when((z2 % 4 != x2) & me)
            def _():
                pltpu.make_async_copy(block, dst, sem).start()

            @pl.when((z2 % 4 != x2) & jnp.logical_not(me))
            def _():
                pltpu.make_async_remote_copy(
                    block, dst, in_send.at[a], sem, device_id=place(y, z2, x2, zhi), device_id_type=MESH
                ).start()

    def wait_bytes(ref, sem):
        pltpu.make_async_copy(ref, ref, sem).wait()

    outs = ((att_s, o_att), (dq_s, o_dq), (dk_s, o_dk), (dv_s, o_dv))

    def send_out(a, h):
        stage, out = outs[a]
        cols = pl.ds(pl.multiple_of(head * HD, HD), HD)

        @pl.loop(0, 8)
        def _(i):
            src = stage.at[pl.ds(pl.multiple_of(h * tile + i * chunk, 16), chunk)]
            dst = out.at[:, cols]
            me = (core == zhi) & (zlo == h) & (i == ten)

            @pl.when(me)
            def _():
                pltpu.make_async_copy(src, dst, out_recv.at[a]).start()

            @pl.when(jnp.logical_not(me))
            def _():
                pltpu.make_async_remote_copy(
                    src, dst, out_send.at[a], out_recv.at[a], device_id=(frame, h, i), device_id_type=MESH
                ).start()

    def forward(a, buf, h):
        for side, has, dev in sides:
            @pl.when(has)
            def _(side=side, dev=dev):
                there = 2 - 2 * side
                pltpu.make_async_remote_copy(
                    buf.at[rows(4 + h)], buf.at[rows(4 * there + h)],
                    halo_send.at[side, a], halo_recv.at[1 - side, a, h], device_id=dev, device_id_type=MESH,
                ).start()

    def give_back(a, ret, got, r):
        for side, has, dev in sides:
            @pl.when(has)
            def _(side=side, dev=dev):
                pltpu.make_async_remote_copy(
                    ret.at[rows(4 * side + r)], got.at[rows(4 * (1 - side) + r)],
                    ret_send.at[side, a], ret_recv.at[1 - side, a, r], device_id=dev, device_id_type=MESH,
                ).start()

    def near_rows(h):
        lo, hi = max(h - 1, 0), min(h + 1, ROWS - 1)
        return lo, hi - lo + 1

    def pairs(h):
        lo, count = near_rows(h)
        return [(f, r) for f in range(3) for r in range(lo, lo + count)]

    def lanes(h, count=1):
        return pl.ds(h * tile, count * tile)

    def seen(h, f, r):
        reach_t, reach_h = ext_ref[h, 0, 0, frame], ext_ref[h, 1, 0, frame]
        inside = (f + frame >= 1) & (f + frame <= FRAMES)
        return inside & (abs(f - 1) <= reach_t) & (abs(r - h) <= reach_h)

    def over_rows(a, fn):
        return fn(a.reshape(tile // 8, 8, tile), axis=0)

    @pl.when(worker)
    def _():
        for side, has, _ in sides:
            @pl.when(jnp.logical_not(has))
            def _(side=side):
                for ref in (kb, vb):
                    ref[rows(8 * side, 4), :] = jnp.zeros((4 * tile, HD), BF)

        for h in range(ROWS):
            wait_bytes(kb.at[rows(4 + h)], in_recv.at[K, h])
            forward(0, kb, h)
        for h in range(ROWS):
            wait_bytes(qb.at[rows(h)], in_recv.at[Q, h])
            qt[:, lanes(h)] = qb[rows(h), :].T
        for side, has, _ in sides:
            @pl.when(has)
            def _(side=side):
                for h in range(ROWS):
                    wait_bytes(kb.at[rows(8 * side + h)], halo_recv.at[side, 0, h])

        inverse = []
        for h in range(ROWS):
            top = jnp.full((8, tile), LOW, F32)
            for f, r in pairs(h):
                s = dot(kb[rows(4 * f + r), :], qt[:, lanes(h)])
                s_all[rows(4 * f + r), :] = s
                top = jnp.maximum(top, jnp.where(seen(h, f, r), over_rows(s, jnp.max), LOW))
            top = jnp.max(top, axis=0, keepdims=True)
            total = jnp.zeros((8, tile), F32)
            for f, r in pairs(h):
                e = jnp.exp2((s_all[rows(4 * f + r), :] - jnp.where(seen(h, f, r), top, HIGH)) * c2)
                e_all[rows(4 * f + r), lanes(h)] = e.astype(BF)
                total = total + over_rows(e, jnp.sum)
            inverse.append(1.0 / jnp.sum(total, axis=0, keepdims=True))

        for h in range(ROWS):
            wait_bytes(vb.at[rows(4 + h)], in_recv.at[V, h])
            forward(1, vb, h)

        def turn(f):
            for h in range(ROWS):
                r = rows(4 * f + h)
                kt[:, r] = kb[r, :].T
                vt[:, r] = vb[r, :].T

        turn(1)
        for side, has, _ in sides:
            @pl.when(has)
            def _(side=side):
                for h in range(ROWS):
                    wait_bytes(vb.at[rows(8 * side + h)], halo_recv.at[side, 1, h])
            turn(2 * side)

        def across(left, right, h):
            lo, count = near_rows(h)
            return sum(
                dot(left[:, rows(4 * f + lo, count)], right[rows(4 * f + lo, count), lanes(h)]) for f in range(3)
            )

        atts = []
        for h in range(ROWS):
            att = (across(vt, e_all, h) * inverse[h]).astype(BF)
            atts.append(att)
            att_s[rows(h), :] = att.T
            send_out(0, h)

        dots = []
        for h in range(ROWS):
            wait_bytes(gb.at[rows(h)], in_recv.at[G, h])
            g = (gb[rows(h), :].T.astype(F32) * inverse[h]).astype(BF)
            gt[:, lanes(h)] = g
            gn[rows(h), :] = g.T
            dots.append(jnp.sum(g.astype(F32) * atts[h].astype(F32), axis=0, keepdims=True))

        def key_term(left, right, f, r):
            lo, count = near_rows(r)
            return dot(left[rows(4 * f + r), lanes(lo, count)], right[rows(lo, count), :])

        for r in range(ROWS):
            for side in range(2):
                dv_ret[rows(4 * side + r), :] = key_term(e_all, gn, 2 * side, r).astype(BF)
            give_back(1, dv_ret, dv_got, r)
        for r in range(ROWS):
            dv_own[rows(r), :] = key_term(e_all, gn, 1, r)

        for h in range(ROWS):
            for f, r in pairs(h):
                dp = dot(vb[rows(4 * f + r), :], gt[:, lanes(h)])
                e = e_all[rows(4 * f + r), lanes(h)].astype(F32)
                ds_all[rows(4 * f + r), lanes(h)] = (e * (dp - dots[h])).astype(BF)
            dq_s[rows(h), :] = (across(kt, ds_all, h) * scale).astype(BF).T
            send_out(1, h)

        for r in range(ROWS):
            for side in range(2):
                dk_ret[rows(4 * side + r), :] = (key_term(ds_all, qb, 2 * side, r) * scale).astype(BF)
            give_back(0, dk_ret, dk_got, r)

        def returned(a, got, r):
            for side, has, _ in sides:
                @pl.when(has)
                def _(side=side):
                    wait_bytes(got.at[rows(4 * side + r)], ret_recv.at[side, a, r])
            return [
                jnp.where(has, got[rows(4 * side + r), :].astype(F32), 0.0) for side, has, _ in sides
            ]

        for r in range(ROWS):
            a, b = returned(1, dv_got, r)
            dv_s[rows(r), :] = (dv_own[rows(r), :] + a + b).astype(BF)
            send_out(3, r)
        for r in range(ROWS):
            own = key_term(ds_all, qb, 1, r) * scale
            a, b = returned(0, dk_got, r)
            dk_s[rows(r), :] = (own + a + b).astype(BF)
            send_out(2, r)

        for side, has, _ in sides:
            @pl.when(has)
            def _(side=side):
                for a in range(2):
                    wait_bytes(kb.at[rows(0, 4)], halo_send.at[side, a])
                    wait_bytes(dk_ret.at[rows(0, 4)], ret_send.at[side, a])

        for a in range(4):
            @pl.when(core == zhi)
            def _(a=a):
                wait_bytes(att_s.at[pl.ds(0, 31 * chunk)], out_send.at[a])

            @pl.when(core != zhi)
            def _(a=a):
                wait_bytes(att_s, out_send.at[a])

    for a in range(4):
        @pl.when(mine)
        def _(a=a):
            wait_bytes(q_ref.at[:, pl.ds(0, 23 * HD)], in_send.at[a])

        @pl.when(jnp.logical_not(mine))
        def _(a=a):
            wait_bytes(q_ref, in_send.at[a])

    for a, (_, out) in enumerate(outs):
        wait_bytes(out, out_recv.at[a])


def settle(*refs):
    for a, b in zip(refs[:4], refs[4:]):
        b[...] = a[...]


def solution(mesh):
    spec = P("tm", "height", None, "tensor", None)

    def shards(query, keys, values, cotangent, extents):
        shape = query.shape
        chunk, width = shape[3], shape[4]
        tile = chunk * mesh.shape["tensor"]
        flat = [a.reshape(chunk, width) for a in (query, keys, values, cotangent)]
        any_spec = pl.BlockSpec(memory_space=pl.ANY)
        four = ROWS * tile
        dma = pltpu.SemaphoreType.DMA
        pieces = [jax.ShapeDtypeStruct((chunk, width), BF)] * 4
        outs = pl.pallas_call(
            functools.partial(kernel, tile, chunk),
            out_shape=pieces,
            in_specs=[pl.BlockSpec(memory_space=pltpu.SMEM)] + [any_spec] * 4,
            out_specs=[any_spec] * 4,
            scratch_shapes=[
                *[pltpu.VMEM((four, HD), BF)] * 2,
                *[pltpu.VMEM((3 * four, HD), BF)] * 2,
                *[pltpu.VMEM((HD, 3 * four), BF)] * 2,
                *[pltpu.VMEM((HD, four), BF)] * 2,
                pltpu.VMEM((four, HD), BF),
                pltpu.VMEM((3 * four, tile), F32),
                *[pltpu.VMEM((3 * four, four), BF)] * 2,
                *[pltpu.VMEM((four, HD), BF)] * 4,
                pltpu.VMEM((four, HD), F32),
                *[pltpu.VMEM((2 * four, HD), BF)] * 4,
                dma((4,)), dma((4, 4)), dma((2, 2)), dma((2, 2, 4)),
                dma((2, 2)), dma((2, 2, 4)), dma((4,)), dma((4,)),
            ],
            compiler_params=pltpu.CompilerParams(
                collective_id=0, has_side_effects=True, vmem_limit_bytes=58 * 2**20
            ),
            name="attention",
        )(jnp.transpose(extents, (1, 3, 2, 0)), *flat)
        outs = pl.pallas_call(settle, out_shape=pieces, name="settle")(*outs)
        return tuple(o.reshape(shape) for o in outs)

    return jax.shard_map(
        shards, mesh=mesh, in_specs=(spec, spec, spec, spec, P()), out_specs=(spec,) * 4, check_vma=False
    )
```

```python
import functools
import math

import jax
import jax.numpy as jnp
from jax import lax
from jax.experimental import pallas as pl
from jax.experimental.pallas import tpu as pltpu
from jax.sharding import PartitionSpec as P

MESH = pl.DeviceIdType.MESH
HD = 128
ROWS = 4
FRAMES = 8
LOW = -1e30
HIGH = 1e30
BF = jnp.bfloat16
F32 = jnp.float32


def dot(a, b):
    return jnp.dot(a, b, preferred_element_type=F32)


def head_of(x, z):
    low = z % 4
    return 6 * x + 3 * (z // 4) + low - (low > x).astype(jnp.int32)


def place(y, z, x, core):
    return (2 * y + z // 4, z % 4, 2 * x + core)


def kernel(
    tile, chunk,
    ext_ref, q_ref, k_ref, v_ref, g_ref,
    o_att, o_dq, o_dk, o_dv,
    qb, gb, kb, vb, kt, vt, qt, gt, gn, s_all, e_all, ds_all,
    att_s, dq_s, dk_s, dv_s, dk_ret, dv_ret, dk_got, dv_got,
    relay_buf,
    in_send, in_recv, halo_send, halo_recv, ret_send, ret_recv, out_send, out_recv, relay_recv,
):
    scale = 1.0 / math.sqrt(HD)
    c2 = scale * math.log2(math.e)
    tm, zlo, ten = (lax.axis_index(a) for a in ("tm", "height", "tensor"))
    y, zhi, x, core = tm // 2, tm % 2, ten // 2, ten % 2
    z = zhi * 4 + zlo
    worker = zlo != x
    frame = 2 * y + core
    mine = worker & (core == zhi)
    has_prev, has_next = frame > 0, frame < FRAMES - 1
    prev_dev = place((frame - 1 + FRAMES) % FRAMES // 2, z, x, 1 - core)
    next_dev = place((frame + 1) % FRAMES // 2, z, x, 1 - core)
    sides = ((0, has_prev, prev_dev), (1, has_next, next_dev))
    head = head_of(x, z)

    def rows(first, count=1):
        return pl.ds(first * tile, count * tile)

    def source(i):
        return (frame, i // 8, i % 8)

    barrier = pltpu.get_barrier_semaphore()

    def greet(dev):
        pl.semaphore_signal(barrier, inc=1, device_id=dev, device_id_type=MESH)

    @pl.when(worker)
    def _():
        @pl.loop(0, 32)
        def _(i):
            me = (core == zhi) & (i // 8 == zlo) & (i % 8 == ten)

            @pl.when(jnp.logical_not(me))
            def _():
                greet(source(i))

        for _, has, dev in sides:
            @pl.when(has)
            def _(dev=dev):
                greet(dev)

    relay_dev = place(y, z, zlo, core)
    own_relay = jnp.logical_not(worker) & (core == zhi)
    for zh in range(2):
        @pl.when(jnp.logical_not(own_relay & (zhi == zh)))
        def _(zh=zh):
            greet((2 * y + zh, x, 2 * x + zhi))

    @pl.when(jnp.logical_not(worker))
    def _():
        for step in range(1, 4):
            greet(place(y, z, (x + step) % 4, core))

    def number(flag):
        return flag.astype(jnp.int32)

    greetings = jnp.where(worker, 25 - number(mine) + number(has_prev) + number(has_next), 32 - number(own_relay))
    pl.semaphore_wait(barrier, greetings)

    K, Q, V, G = range(4)
    arrays = ((k_ref, kb, 4), (q_ref, qb, 0), (v_ref, vb, 4), (g_ref, gb, 0))

    def put(first):
        return pl.ds(pl.multiple_of(first * tile + ten * chunk, 16), chunk)

    for a, (src, buf, first) in enumerate(arrays):
        @pl.loop(0, 32)
        def _(i, a=a, src=src, buf=buf, first=first):
            x2, z2 = (x + i // 8) % 4, (z + i % 8) % 8
            block = src.at[:, pl.ds(pl.multiple_of(head_of(x2, z2) * HD, HD), HD)]
            dst = buf.at[put(first + zlo)]
            sem = in_recv.at[a, i // 8]
            me = (i == 0) & (core == zhi)

            @pl.when((z2 % 4 != x2) & me)
            def _():
                pltpu.make_async_copy(block, dst, sem).start()

            @pl.when((z2 % 4 != x2) & jnp.logical_not(me))
            def _():
                pltpu.make_async_remote_copy(
                    block, dst, in_send.at[a], sem, device_id=place(y, z2, x2, zhi), device_id_type=MESH
                ).start()

    def wait_bytes(ref, sem):
        pltpu.make_async_copy(ref, ref, sem).wait()

    outs = ((att_s, o_att), (dq_s, o_dq), (dk_s, o_dk), (dv_s, o_dv))

    def columns(which):
        return pl.ds(pl.multiple_of(which * HD, HD), HD)

    def slot(a, who, h):
        return pl.ds(pl.multiple_of(((a * 4 + who) * ROWS + h) * 2 * chunk, 16), 2 * chunk)

    def send_out(a, row=None):
        stage, out = outs[a]
        count = ROWS if row is None else 1

        def which(i):
            return (i + zlo) % ROWS if row is None else row

        @pl.loop(0, count)
        def _(i):
            h = which(i)
            first = pl.multiple_of(h * tile + 2 * zlo * chunk, 16)
            pltpu.make_async_remote_copy(
                stage.at[pl.ds(first, 2 * chunk)], relay_buf.at[slot(a, x, h)], out_send.at[a],
                relay_recv.at[a, x, h], device_id=relay_dev, device_id_type=MESH,
            ).start()

        @pl.loop(0, 6 * count)
        def _(i):
            h, piece = which(i // 6), (2 * zlo + 2 + i % 6) % 8
            first = pl.multiple_of(h * tile + piece * chunk, 16)
            me = (core == zhi) & (zlo == h) & (piece == ten)

            @pl.when(me)
            def _():
                pltpu.make_async_copy(stage.at[pl.ds(first, chunk)], out.at[:, columns(head)], out_recv.at[a]).start()

            @pl.when(jnp.logical_not(me))
            def _():
                pltpu.make_async_remote_copy(
                    stage.at[pl.ds(first, chunk)], out.at[:, columns(head)], out_send.at[a], out_recv.at[a],
                    device_id=(frame, h, piece), device_id_type=MESH,
                ).start()

    def pass_on(a):
        _, out = outs[a]

        @pl.loop(0, 12)
        def _(i):
            h, who = (i // 3 + (zlo if a > 1 else 0)) % ROWS, (x + 1 + i % 3) % 4
            wait_bytes(relay_buf.at[slot(a, who, h)], relay_recv.at[a, who, h])
            base = pl.multiple_of(((a * 4 + who) * ROWS + h) * 2 * chunk, 16)
            cols = columns(head_of(who, z))
            for s in range(2):
                src = relay_buf.at[pl.ds(base + s * chunk, chunk)]
                me = (core == zhi) & (h == zlo) & (core == s)

                @pl.when(me)
                def _(src=src):
                    pltpu.make_async_copy(src, out.at[:, cols], out_recv.at[a]).start()

                @pl.when(jnp.logical_not(me))
                def _(src=src, s=s):
                    pltpu.make_async_remote_copy(
                        src, out.at[:, cols], out_send.at[a], out_recv.at[a],
                        device_id=(frame, h, 2 * x + s), device_id_type=MESH,
                    ).start()

    def forward(a, buf, d):
        piece = (x - d + 4) % 4 * 2 * chunk
        for side, has, dev in sides:
            @pl.when(has)
            def _(side=side, dev=dev):
                there = 2 - 2 * side
                for h in range(ROWS):
                    pltpu.make_async_remote_copy(
                        buf.at[pl.ds(pl.multiple_of((4 + h) * tile + piece, 16), 2 * chunk)],
                        buf.at[pl.ds(pl.multiple_of((4 * there + h) * tile + piece, 16), 2 * chunk)],
                        halo_send.at[side, a], halo_recv.at[1 - side, a], device_id=dev, device_id_type=MESH,
                    ).start()

    def arrived(a, d):
        wait_bytes(qb.at[rows(0)], in_recv.at[a, d])

    def halo_arrived(a, buf):
        for side, has, _ in sides:
            @pl.when(has)
            def _(side=side):
                wait_bytes(buf.at[rows(8 * side, 4)], halo_recv.at[side, a])

    def give_back(a, ret, got, r):
        for side, has, dev in sides:
            @pl.when(has)
            def _(side=side, dev=dev):
                pltpu.make_async_remote_copy(
                    ret.at[rows(4 * side + r)], got.at[rows(4 * (1 - side) + r)],
                    ret_send.at[side, a], ret_recv.at[1 - side, a, r], device_id=dev, device_id_type=MESH,
                ).start()

    def near_rows(h):
        lo, hi = max(h - 1, 0), min(h + 1, ROWS - 1)
        return lo, hi - lo + 1

    def pairs(h):
        lo, count = near_rows(h)
        return [(f, r) for f in range(3) for r in range(lo, lo + count)]

    def lanes(h, count=1):
        return pl.ds(h * tile, count * tile)

    def seen(h, f, r):
        reach_t, reach_h = ext_ref[h, 0, 0, frame], ext_ref[h, 1, 0, frame]
        inside = (f + frame >= 1) & (f + frame <= FRAMES)
        return inside & (abs(f - 1) <= reach_t) & (abs(r - h) <= reach_h)

    def over_rows(a, fn):
        return fn(a.reshape(tile // 8, 8, tile), axis=0)

    @pl.when(worker)
    def _():
        for side, has, _ in sides:
            @pl.when(jnp.logical_not(has))
            def _(side=side):
                for ref in (kb, vb):
                    ref[rows(8 * side, 4), :] = jnp.zeros((4 * tile, HD), BF)

        for d in range(4):
            arrived(K, d)
            forward(0, kb, d)
        for d in range(4):
            arrived(Q, d)
        for h in range(ROWS):
            qt[:, lanes(h)] = qb[rows(h), :].T
        halo_arrived(0, kb)

        inverse = []
        for h in range(ROWS):
            top = jnp.full((8, tile), LOW, F32)
            for f, r in pairs(h):
                s = dot(kb[rows(4 * f + r), :], qt[:, lanes(h)])
                s_all[rows(4 * f + r), :] = s
                top = jnp.maximum(top, jnp.where(seen(h, f, r), over_rows(s, jnp.max), LOW))
            top = jnp.max(top, axis=0, keepdims=True)
            total = jnp.zeros((8, tile), F32)
            for f, r in pairs(h):
                e = jnp.exp2((s_all[rows(4 * f + r), :] - jnp.where(seen(h, f, r), top, HIGH)) * c2)
                e_all[rows(4 * f + r), lanes(h)] = e.astype(BF)
                total = total + over_rows(e, jnp.sum)
            inverse.append(1.0 / jnp.sum(total, axis=0, keepdims=True))

        for d in range(4):
            arrived(V, d)
            forward(1, vb, d)

        def turn(to, buf, f):
            for h in range(ROWS):
                r = rows(4 * f + h)
                to[:, r] = buf[r, :].T

        turn(vt, vb, 1)
        for f in range(3):
            turn(kt, kb, f)
        halo_arrived(1, vb)
        turn(vt, vb, 0)
        turn(vt, vb, 2)

        def across(left, right, h):
            lo, count = near_rows(h)
            return sum(
                dot(left[:, rows(4 * f + lo, count)], right[rows(4 * f + lo, count), lanes(h)]) for f in range(3)
            )

        atts = []
        for h in range(ROWS):
            att = (across(vt, e_all, h) * inverse[h]).astype(BF)
            atts.append(att)
            att_s[rows(h), :] = att.T
            send_out(0, h)

        dots = []
        for d in range(4):
            arrived(G, d)
        for h in range(ROWS):
            g = (gb[rows(h), :].T.astype(F32) * inverse[h]).astype(BF)
            gt[:, lanes(h)] = g
            gn[rows(h), :] = g.T
            dots.append(jnp.sum(g.astype(F32) * atts[h].astype(F32), axis=0, keepdims=True))

        def key_term(left, right, f, r):
            lo, count = near_rows(r)
            return dot(left[rows(4 * f + r), lanes(lo, count)], right[rows(lo, count), :])

        for r in range(ROWS):
            for side in range(2):
                dv_ret[rows(4 * side + r), :] = key_term(e_all, gn, 2 * side, r).astype(BF)
            give_back(1, dv_ret, dv_got, r)
        for h in range(ROWS):
            for f, r in pairs(h):
                dp = dot(vb[rows(4 * f + r), :], gt[:, lanes(h)])
                e = e_all[rows(4 * f + r), lanes(h)].astype(F32)
                ds_all[rows(4 * f + r), lanes(h)] = (e * (dp - dots[h])).astype(BF)
            dq_s[rows(h), :] = (across(kt, ds_all, h) * scale).astype(BF).T
            send_out(1, h)

        for r in range(ROWS):
            for side in range(2):
                dk_ret[rows(4 * side + r), :] = (key_term(ds_all, qb, 2 * side, r) * scale).astype(BF)
            give_back(0, dk_ret, dk_got, r)

        def returned(a, got, r):
            for side, has, _ in sides:
                @pl.when(has)
                def _(side=side):
                    wait_bytes(got.at[rows(4 * side + r)], ret_recv.at[side, a, r])
            return [
                jnp.where(has, got[rows(4 * side + r), :].astype(F32), 0.0) for side, has, _ in sides
            ]

        for r in range(ROWS):
            a, b = returned(1, dv_got, r)
            dv_s[rows(r), :] = (key_term(e_all, gn, 1, r) + a + b).astype(BF)
        send_out(3)
        for r in range(ROWS):
            own = key_term(ds_all, qb, 1, r) * scale
            a, b = returned(0, dk_got, r)
            dk_s[rows(r), :] = (own + a + b).astype(BF)
        send_out(2)

        for side, has, _ in sides:
            @pl.when(has)
            def _(side=side):
                for a in range(2):
                    wait_bytes(kb.at[rows(0, 4)], halo_send.at[side, a])
                    wait_bytes(dk_ret.at[rows(0, 4)], ret_send.at[side, a])

        for a in range(4):
            @pl.when(core == zhi)
            def _(a=a):
                wait_bytes(att_s.at[pl.ds(0, 31 * chunk)], out_send.at[a])

            @pl.when(core != zhi)
            def _(a=a):
                wait_bytes(att_s, out_send.at[a])

    @pl.when(jnp.logical_not(worker))
    def _():
        for a in (0, 1, 3, 2):
            pass_on(a)
        for a in range(4):
            @pl.when(core == zhi)
            def _(a=a):
                wait_bytes(relay_buf.at[pl.ds(0, 21 * chunk)], out_send.at[a])

            @pl.when(core != zhi)
            def _(a=a):
                wait_bytes(relay_buf.at[pl.ds(0, 24 * chunk)], out_send.at[a])

    for a in range(4):
        @pl.when(mine)
        def _(a=a):
            wait_bytes(q_ref.at[:, pl.ds(0, 23 * HD)], in_send.at[a])

        @pl.when(jnp.logical_not(mine))
        def _(a=a):
            wait_bytes(q_ref, in_send.at[a])

    for a, (_, out) in enumerate(outs):
        wait_bytes(out, out_recv.at[a])


def settle(*refs):
    for a, b in zip(refs[:4], refs[4:]):
        b[...] = a[...]


def solution(mesh):
    spec = P("tm", "height", None, "tensor", None)

    def shards(query, keys, values, cotangent, extents):
        shape = query.shape
        chunk, width = shape[3], shape[4]
        tile = chunk * mesh.shape["tensor"]
        flat = [a.reshape(chunk, width) for a in (query, keys, values, cotangent)]
        any_spec = pl.BlockSpec(memory_space=pl.ANY)
        four = ROWS * tile
        dma = pltpu.SemaphoreType.DMA
        pieces = [jax.ShapeDtypeStruct((chunk, width), BF)] * 4
        outs = pl.pallas_call(
            functools.partial(kernel, tile, chunk),
            out_shape=pieces,
            in_specs=[pl.BlockSpec(memory_space=pltpu.SMEM)] + [any_spec] * 4,
            out_specs=[any_spec] * 4,
            scratch_shapes=[
                *[pltpu.VMEM((four, HD), BF)] * 2,
                *[pltpu.VMEM((3 * four, HD), BF)] * 2,
                *[pltpu.VMEM((HD, 3 * four), BF)] * 2,
                *[pltpu.VMEM((HD, four), BF)] * 2,
                pltpu.VMEM((four, HD), BF),
                pltpu.VMEM((3 * four, tile), F32),
                *[pltpu.VMEM((3 * four, four), BF)] * 2,
                *[pltpu.VMEM((four, HD), BF)] * 4,
                *[pltpu.VMEM((2 * four, HD), BF)] * 4,
                pltpu.VMEM((4 * 4 * ROWS * 2 * chunk, HD), BF),
                dma((4,)), dma((4, 4)), dma((2, 2)), dma((2, 2)),
                dma((2, 2)), dma((2, 2, 4)), dma((4,)), dma((4,)), dma((4, 4, ROWS)),
            ],
            compiler_params=pltpu.CompilerParams(
                collective_id=0, has_side_effects=True, vmem_limit_bytes=58 * 2**20
            ),
            name="attention",
        )(jnp.transpose(extents, (1, 3, 2, 0)), *flat)
        outs = pl.pallas_call(settle, out_shape=pieces, name="settle")(*outs)
        return tuple(o.reshape(shape) for o in outs)

    return jax.shard_map(
        shards, mesh=mesh, in_specs=(spec, spec, spec, spec, P()), out_specs=(spec,) * 4, check_vma=False
    )
```

```python
import functools
import math

import jax
import jax.numpy as jnp
from jax import lax
from jax.experimental import pallas as pl
from jax.experimental.pallas import tpu as pltpu
from jax.sharding import PartitionSpec as P

MESH = pl.DeviceIdType.MESH
HD = 128
ROWS = 4
FRAMES = 8
LOW = -1e30
HIGH = 1e30
BF = jnp.bfloat16
F32 = jnp.float32


def dot(a, b):
    return jnp.dot(a, b, preferred_element_type=F32)


def head_of(x, z):
    low = z % 4
    return 6 * x + 3 * (z // 4) + low - (low > x).astype(jnp.int32)


def place(y, z, x, core):
    return (2 * y + z // 4, z % 4, 2 * x + core)


def kernel(
    tile, chunk,
    ext_ref, q_ref, k_ref, v_ref, g_ref,
    o_att, o_dq, o_dk, o_dv,
    qb, gb, kb, vb, kt, vt, qt, gt, gn, s_all, e_all, ds_all,
    att_s, dq_s, dk_s, dv_s, dk_ret, dv_ret, dk_got, dv_got,
    relay_buf,
    in_send, in_recv, halo_send, halo_recv, ret_send, ret_recv, out_send, out_recv, relay_recv,
):
    scale = 1.0 / math.sqrt(HD)
    c2 = scale * math.log2(math.e)
    tm, zlo, ten = (lax.axis_index(a) for a in ("tm", "height", "tensor"))
    y, zhi, x, core = tm // 2, tm % 2, ten // 2, ten % 2
    z = zhi * 4 + zlo
    worker = zlo != x
    frame = 2 * y + core
    mine = worker & (core == zhi)
    has_prev, has_next = frame > 0, frame < FRAMES - 1
    prev_dev = place((frame - 1 + FRAMES) % FRAMES // 2, z, x, 1 - core)
    next_dev = place((frame + 1) % FRAMES // 2, z, x, 1 - core)
    sides = ((0, has_prev, prev_dev), (1, has_next, next_dev))
    head = head_of(x, z)

    def rows(first, count=1):
        return pl.ds(first * tile, count * tile)

    def source(i):
        return (frame, i // 8, i % 8)

    barrier = pltpu.get_barrier_semaphore()

    def greet(dev):
        pl.semaphore_signal(barrier, inc=1, device_id=dev, device_id_type=MESH)

    @pl.when(worker)
    def _():
        @pl.loop(0, 32)
        def _(i):
            me = (core == zhi) & (i // 8 == zlo) & (i % 8 == ten)

            @pl.when(jnp.logical_not(me))
            def _():
                greet(source(i))

        for _, has, dev in sides:
            @pl.when(has)
            def _(dev=dev):
                greet(dev)

    relay_dev = place(y, z, zlo, core)
    own_relay = jnp.logical_not(worker) & (core == zhi)
    for zh in range(2):
        @pl.when(jnp.logical_not(own_relay & (zhi == zh)))
        def _(zh=zh):
            greet((2 * y + zh, x, 2 * x + zhi))

    @pl.when(jnp.logical_not(worker))
    def _():
        for step in range(1, 4):
            greet(place(y, z, (x + step) % 4, core))

    def number(flag):
        return flag.astype(jnp.int32)

    greetings = jnp.where(worker, 25 - number(mine) + number(has_prev) + number(has_next), 32 - number(own_relay))
    pl.semaphore_wait(barrier, greetings)

    K, Q, V, G = range(4)
    arrays = ((k_ref, kb, 4), (q_ref, qb, 0), (v_ref, vb, 4), (g_ref, gb, 0))

    def put(first):
        return pl.ds(pl.multiple_of(first * tile + ten * chunk, 16), chunk)

    for a, (src, buf, first) in enumerate(arrays):
        @pl.loop(0, 32)
        def _(i, a=a, src=src, buf=buf, first=first):
            x2, z2 = (x + i // 8) % 4, (z + i % 8) % 8
            block = src.at[:, pl.ds(pl.multiple_of(head_of(x2, z2) * HD, HD), HD)]
            dst = buf.at[put(first + zlo)]
            sem = in_recv.at[a, i // 8]
            me = (i == 0) & (core == zhi)

            @pl.when((z2 % 4 != x2) & me)
            def _():
                pltpu.make_async_copy(block, dst, sem).start()

            @pl.when((z2 % 4 != x2) & jnp.logical_not(me))
            def _():
                pltpu.make_async_remote_copy(
                    block, dst, in_send.at[a], sem, device_id=place(y, z2, x2, zhi), device_id_type=MESH
                ).start()

    def wait_bytes(ref, sem):
        pltpu.make_async_copy(ref, ref, sem).wait()

    outs = ((att_s, o_att), (dq_s, o_dq), (dk_s, o_dk), (dv_s, o_dv))

    def columns(which):
        return pl.ds(pl.multiple_of(which * HD, HD), HD)

    def slot(a, who, h):
        return pl.ds(pl.multiple_of(((a * 4 + who) * ROWS + h) * 2 * chunk, 16), 2 * chunk)

    def send_out(a, row=None):
        stage, out = outs[a]
        count = ROWS if row is None else 1

        def which(i):
            return (i + zlo) % ROWS if row is None else row

        @pl.loop(0, count)
        def _(i):
            h = which(i)
            first = pl.multiple_of(h * tile + 2 * zlo * chunk, 16)
            pltpu.make_async_remote_copy(
                stage.at[pl.ds(first, 2 * chunk)], relay_buf.at[slot(a, x, h)], out_send.at[a],
                relay_recv.at[a, x, h], device_id=relay_dev, device_id_type=MESH,
            ).start()

        @pl.loop(0, 6 * count)
        def _(i):
            h, piece = which(i // 6), (2 * zlo + 2 + i % 6) % 8
            first = pl.multiple_of(h * tile + piece * chunk, 16)
            me = (core == zhi) & (zlo == h) & (piece == ten)

            @pl.when(me)
            def _():
                pltpu.make_async_copy(stage.at[pl.ds(first, chunk)], out.at[:, columns(head)], out_recv.at[a]).start()

            @pl.when(jnp.logical_not(me))
            def _():
                pltpu.make_async_remote_copy(
                    stage.at[pl.ds(first, chunk)], out.at[:, columns(head)], out_send.at[a], out_recv.at[a],
                    device_id=(frame, h, piece), device_id_type=MESH,
                ).start()

    def pass_on(a):
        _, out = outs[a]

        @pl.loop(0, 12)
        def _(i):
            h, who = i // 3, (x + 1 + i % 3) % 4
            wait_bytes(relay_buf.at[slot(a, who, h)], relay_recv.at[a, who, h])
            base = pl.multiple_of(((a * 4 + who) * ROWS + h) * 2 * chunk, 16)
            cols = columns(head_of(who, z))
            for s in range(2):
                src = relay_buf.at[pl.ds(base + s * chunk, chunk)]
                me = (core == zhi) & (h == zlo) & (core == s)

                @pl.when(me)
                def _(src=src):
                    pltpu.make_async_copy(src, out.at[:, cols], out_recv.at[a]).start()

                @pl.when(jnp.logical_not(me))
                def _(src=src, s=s):
                    pltpu.make_async_remote_copy(
                        src, out.at[:, cols], out_send.at[a], out_recv.at[a],
                        device_id=(frame, h, 2 * x + s), device_id_type=MESH,
                    ).start()

    def forward(a, buf, d):
        piece = (x - d + 4) % 4 * 2 * chunk
        for side, has, dev in sides:
            @pl.when(has)
            def _(side=side, dev=dev):
                there = 2 - 2 * side
                for h in range(ROWS):
                    pltpu.make_async_remote_copy(
                        buf.at[pl.ds(pl.multiple_of((4 + h) * tile + piece, 16), 2 * chunk)],
                        buf.at[pl.ds(pl.multiple_of((4 * there + h) * tile + piece, 16), 2 * chunk)],
                        halo_send.at[side, a], halo_recv.at[1 - side, a], device_id=dev, device_id_type=MESH,
                    ).start()

    def arrived(a, d):
        wait_bytes(qb.at[rows(0)], in_recv.at[a, d])

    def halo_arrived(a, buf):
        for side, has, _ in sides:
            @pl.when(has)
            def _(side=side):
                wait_bytes(buf.at[rows(8 * side, 4)], halo_recv.at[side, a])

    def give_back(a, ret, got, r):
        for side, has, dev in sides:
            @pl.when(has)
            def _(side=side, dev=dev):
                pltpu.make_async_remote_copy(
                    ret.at[rows(4 * side + r)], got.at[rows(4 * (1 - side) + r)],
                    ret_send.at[side, a], ret_recv.at[1 - side, a, r], device_id=dev, device_id_type=MESH,
                ).start()

    def near_rows(h):
        lo, hi = max(h - 1, 0), min(h + 1, ROWS - 1)
        return lo, hi - lo + 1

    def pairs(h):
        lo, count = near_rows(h)
        return [(f, r) for f in range(3) for r in range(lo, lo + count)]

    def lanes(h, count=1):
        return pl.ds(h * tile, count * tile)

    def seen(h, f, r):
        reach_t, reach_h = ext_ref[h, 0, 0, frame], ext_ref[h, 1, 0, frame]
        inside = (f + frame >= 1) & (f + frame <= FRAMES)
        return inside & (abs(f - 1) <= reach_t) & (abs(r - h) <= reach_h)

    def over_rows(a, fn):
        return fn(a.reshape(tile // 8, 8, tile), axis=0)

    @pl.when(worker)
    def _():
        for side, has, _ in sides:
            @pl.when(jnp.logical_not(has))
            def _(side=side):
                for ref in (kb, vb):
                    ref[rows(8 * side, 4), :] = jnp.zeros((4 * tile, HD), BF)

        for d in range(4):
            arrived(K, d)
            forward(0, kb, d)
        for d in range(4):
            arrived(Q, d)
        for h in range(ROWS):
            qt[:, lanes(h)] = qb[rows(h), :].T
        halo_arrived(0, kb)

        inverse = []
        for h in range(ROWS):
            top = jnp.full((8, tile), LOW, F32)
            for f, r in pairs(h):
                s = dot(kb[rows(4 * f + r), :], qt[:, lanes(h)])
                s_all[rows(4 * f + r), :] = s
                top = jnp.maximum(top, jnp.where(seen(h, f, r), over_rows(s, jnp.max), LOW))
            top = jnp.max(top, axis=0, keepdims=True)
            total = jnp.zeros((8, tile), F32)
            for f, r in pairs(h):
                e = jnp.exp2((s_all[rows(4 * f + r), :] - jnp.where(seen(h, f, r), top, HIGH)) * c2)
                e_all[rows(4 * f + r), lanes(h)] = e.astype(BF)
                total = total + over_rows(e, jnp.sum)
            inverse.append(1.0 / jnp.sum(total, axis=0, keepdims=True))

        for d in range(4):
            arrived(V, d)
            forward(1, vb, d)

        def turn(to, buf, f):
            for h in range(ROWS):
                r = rows(4 * f + h)
                to[:, r] = buf[r, :].T

        turn(vt, vb, 1)
        for f in range(3):
            turn(kt, kb, f)
        halo_arrived(1, vb)
        turn(vt, vb, 0)
        turn(vt, vb, 2)

        def across(left, right, h):
            lo, count = near_rows(h)
            return sum(
                dot(left[:, rows(4 * f + lo, count)], right[rows(4 * f + lo, count), lanes(h)]) for f in range(3)
            )

        atts = []
        for h in range(ROWS):
            att = (across(vt, e_all, h) * inverse[h]).astype(BF)
            atts.append(att)
            att_s[rows(h), :] = att.T
            send_out(0, h)

        dots = []
        for d in range(4):
            arrived(G, d)
        for h in range(ROWS):
            g = (gb[rows(h), :].T.astype(F32) * inverse[h]).astype(BF)
            gt[:, lanes(h)] = g
            gn[rows(h), :] = g.T
            dots.append(jnp.sum(g.astype(F32) * atts[h].astype(F32), axis=0, keepdims=True))

        def key_term(left, right, f, r):
            lo, count = near_rows(r)
            return dot(left[rows(4 * f + r), lanes(lo, count)], right[rows(lo, count), :])

        for r in range(ROWS):
            for side in range(2):
                dv_ret[rows(4 * side + r), :] = key_term(e_all, gn, 2 * side, r).astype(BF)
            give_back(1, dv_ret, dv_got, r)
        for h in range(ROWS):
            for f, r in pairs(h):
                dp = dot(vb[rows(4 * f + r), :], gt[:, lanes(h)])
                e = e_all[rows(4 * f + r), lanes(h)].astype(F32)
                ds_all[rows(4 * f + r), lanes(h)] = (e * (dp - dots[h])).astype(BF)
            dq_s[rows(h), :] = (across(kt, ds_all, h) * scale).astype(BF).T
            send_out(1, h)

        for r in range(ROWS):
            for side in range(2):
                dk_ret[rows(4 * side + r), :] = (key_term(ds_all, qb, 2 * side, r) * scale).astype(BF)
            give_back(0, dk_ret, dk_got, r)

        def returned(a, got, r):
            for side, has, _ in sides:
                @pl.when(has)
                def _(side=side):
                    wait_bytes(got.at[rows(4 * side + r)], ret_recv.at[side, a, r])
            return [
                jnp.where(has, got[rows(4 * side + r), :].astype(F32), 0.0) for side, has, _ in sides
            ]

        for r in range(ROWS):
            a, b = returned(1, dv_got, r)
            dv_s[rows(r), :] = (key_term(e_all, gn, 1, r) + a + b).astype(BF)
            send_out(3, r)
        for r in range(ROWS):
            own = key_term(ds_all, qb, 1, r) * scale
            a, b = returned(0, dk_got, r)
            dk_s[rows(r), :] = (own + a + b).astype(BF)
            send_out(2, r)

        for side, has, _ in sides:
            @pl.when(has)
            def _(side=side):
                for a in range(2):
                    wait_bytes(kb.at[rows(0, 4)], halo_send.at[side, a])
                    wait_bytes(dk_ret.at[rows(0, 4)], ret_send.at[side, a])

        for a in range(4):
            @pl.when(core == zhi)
            def _(a=a):
                wait_bytes(att_s.at[pl.ds(0, 31 * chunk)], out_send.at[a])

            @pl.when(core != zhi)
            def _(a=a):
                wait_bytes(att_s, out_send.at[a])

    @pl.when(jnp.logical_not(worker))
    def _():
        for a in (0, 1, 3, 2):
            pass_on(a)
        for a in range(4):
            @pl.when(core == zhi)
            def _(a=a):
                wait_bytes(relay_buf.at[pl.ds(0, 21 * chunk)], out_send.at[a])

            @pl.when(core != zhi)
            def _(a=a):
                wait_bytes(relay_buf.at[pl.ds(0, 24 * chunk)], out_send.at[a])

    for a in range(4):
        @pl.when(mine)
        def _(a=a):
            wait_bytes(q_ref.at[:, pl.ds(0, 23 * HD)], in_send.at[a])

        @pl.when(jnp.logical_not(mine))
        def _(a=a):
            wait_bytes(q_ref, in_send.at[a])

    for a, (_, out) in enumerate(outs):
        wait_bytes(out, out_recv.at[a])


def settle(*refs):
    froms, tos, held, loaded, stored = refs[:4], refs[4:8], refs[8:12], refs[12], refs[13]
    loads = [pltpu.make_async_copy(a, b, loaded.at[i]) for i, (a, b) in enumerate(zip(froms, held))]
    stores = [pltpu.make_async_copy(a, b, stored.at[i]) for i, (a, b) in enumerate(zip(held, tos))]
    for load in loads:
        load.start()
    for load, store in zip(loads, stores):
        load.wait()
        store.start()
    for store in stores:
        store.wait()


def solution(mesh):
    spec = P("tm", "height", None, "tensor", None)

    def shards(query, keys, values, cotangent, extents):
        shape = query.shape
        chunk, width = shape[3], shape[4]
        tile = chunk * mesh.shape["tensor"]
        flat = [a.reshape(chunk, width) for a in (query, keys, values, cotangent)]
        any_spec = pl.BlockSpec(memory_space=pl.ANY)
        four = ROWS * tile
        dma = pltpu.SemaphoreType.DMA
        pieces = [jax.ShapeDtypeStruct((chunk, width), BF)] * 4
        outs = pl.pallas_call(
            functools.partial(kernel, tile, chunk),
            out_shape=pieces,
            in_specs=[pl.BlockSpec(memory_space=pltpu.SMEM)] + [any_spec] * 4,
            out_specs=[any_spec] * 4,
            scratch_shapes=[
                *[pltpu.VMEM((four, HD), BF)] * 2,
                *[pltpu.VMEM((3 * four, HD), BF)] * 2,
                *[pltpu.VMEM((HD, 3 * four), BF)] * 2,
                *[pltpu.VMEM((HD, four), BF)] * 2,
                pltpu.VMEM((four, HD), BF),
                pltpu.VMEM((3 * four, tile), F32),
                *[pltpu.VMEM((3 * four, four), BF)] * 2,
                *[pltpu.VMEM((four, HD), BF)] * 4,
                *[pltpu.VMEM((2 * four, HD), BF)] * 4,
                pltpu.VMEM((4 * 4 * ROWS * 2 * chunk, HD), BF),
                dma((4,)), dma((4, 4)), dma((2, 2)), dma((2, 2)),
                dma((2, 2)), dma((2, 2, 4)), dma((4,)), dma((4,)), dma((4, 4, ROWS)),
            ],
            compiler_params=pltpu.CompilerParams(
                collective_id=0, has_side_effects=True, vmem_limit_bytes=58 * 2**20
            ),
            name="attention",
        )(jnp.transpose(extents, (1, 3, 2, 0)), *flat)
        outs = pl.pallas_call(
            settle,
            out_shape=pieces,
            in_specs=[any_spec] * 4,
            out_specs=[any_spec] * 4,
            scratch_shapes=[*[pltpu.VMEM((chunk, width), BF)] * 4, dma((4,)), dma((4,))],
            compiler_params=pltpu.CompilerParams(vmem_limit_bytes=58 * 2**20),
            name="settle",
        )(*outs)
        return tuple(o.reshape(shape) for o in outs)

    return jax.shard_map(
        shards, mesh=mesh, in_specs=(spec, spec, spec, spec, P()), out_specs=(spec,) * 4, check_vma=False
    )
```

```python
import functools
import math

import jax
import jax.numpy as jnp
from jax import lax
from jax.experimental import pallas as pl
from jax.experimental.pallas import tpu as pltpu
from jax.sharding import PartitionSpec as P

MESH = pl.DeviceIdType.MESH
HD = 128
ROWS = 4
FRAMES = 8
LOW = -1e30
HIGH = 1e30
BF = jnp.bfloat16
F32 = jnp.float32


def dot(a, b):
    return jnp.dot(a, b, preferred_element_type=F32)


def head_of(x, z):
    low = z % 4
    return 6 * x + 3 * (z // 4) + low - (low > x).astype(jnp.int32)


def place(y, z, x, core):
    return (2 * y + z // 4, z % 4, 2 * x + core)


def kernel(
    tile, chunk,
    ext_ref, q_ref, k_ref, v_ref, g_ref,
    o_att, o_dq, o_dk, o_dv,
    qb, gb, kb, vb, kt, vt, qt, gt, gn, s_all, e_all, ds_all,
    att_s, dq_s, dk_s, dv_s, dk_ret, dv_ret, dk_got, dv_got,
    relay_buf,
    in_send, in_recv, halo_send, halo_recv, ret_send, ret_recv, out_send, out_recv, relay_recv,
):
    scale = 1.0 / math.sqrt(HD)
    c2 = scale * math.log2(math.e)
    tm, zlo, ten = (lax.axis_index(a) for a in ("tm", "height", "tensor"))
    y, zhi, x, core = tm // 2, tm % 2, ten // 2, ten % 2
    z = zhi * 4 + zlo
    worker = zlo != x
    frame = 2 * y + core
    mine = worker & (core == zhi)
    has_prev, has_next = frame > 0, frame < FRAMES - 1
    prev_dev = place((frame - 1 + FRAMES) % FRAMES // 2, z, x, 1 - core)
    next_dev = place((frame + 1) % FRAMES // 2, z, x, 1 - core)
    sides = ((0, has_prev, prev_dev), (1, has_next, next_dev))
    head = head_of(x, z)

    def rows(first, count=1):
        return pl.ds(first * tile, count * tile)

    def source(i):
        return (frame, i // 8, i % 8)

    barrier = pltpu.get_barrier_semaphore()

    def greet(dev):
        pl.semaphore_signal(barrier, inc=1, device_id=dev, device_id_type=MESH)

    @pl.when(worker)
    def _():
        @pl.loop(0, 32)
        def _(i):
            me = (core == zhi) & (i // 8 == zlo) & (i % 8 == ten)

            @pl.when(jnp.logical_not(me))
            def _():
                greet(source(i))

        for _, has, dev in sides:
            @pl.when(has)
            def _(dev=dev):
                greet(dev)

    relay_dev = place(y, z, zlo, core)
    own_relay = jnp.logical_not(worker) & (core == zhi)
    for zh in range(2):
        @pl.when(jnp.logical_not(own_relay & (zhi == zh)))
        def _(zh=zh):
            greet((2 * y + zh, x, 2 * x + zhi))

    @pl.when(jnp.logical_not(worker))
    def _():
        for step in range(1, 4):
            greet(place(y, z, (x + step) % 4, core))

    def number(flag):
        return flag.astype(jnp.int32)

    greetings = jnp.where(worker, 25 - number(mine) + number(has_prev) + number(has_next), 32 - number(own_relay))
    pl.semaphore_wait(barrier, greetings)

    K, Q, V, G = range(4)
    arrays = ((k_ref, kb, 4), (q_ref, qb, 0), (v_ref, vb, 4), (g_ref, gb, 0))

    def put(first):
        return pl.ds(pl.multiple_of(first * tile + ten * chunk, 16), chunk)

    for a, (src, buf, first) in enumerate(arrays):
        @pl.loop(0, 32)
        def _(i, a=a, src=src, buf=buf, first=first):
            x2, z2 = (x + i // 8) % 4, (z + i % 8) % 8
            block = src.at[:, pl.ds(pl.multiple_of(head_of(x2, z2) * HD, HD), HD)]
            dst = buf.at[put(first + zlo)]
            sem = in_recv.at[a, i // 8]
            me = (i == 0) & (core == zhi)

            @pl.when((z2 % 4 != x2) & me)
            def _():
                pltpu.make_async_copy(block, dst, sem).start()

            @pl.when((z2 % 4 != x2) & jnp.logical_not(me))
            def _():
                pltpu.make_async_remote_copy(
                    block, dst, in_send.at[a], sem, device_id=place(y, z2, x2, zhi), device_id_type=MESH
                ).start()

    def wait_bytes(ref, sem):
        pltpu.make_async_copy(ref, ref, sem).wait()

    outs = ((att_s, o_att), (dq_s, o_dq), (dk_s, o_dk), (dv_s, o_dv))

    def columns(which):
        return pl.ds(pl.multiple_of(which * HD, HD), HD)

    def slot(a, who, h):
        return pl.ds(pl.multiple_of(((a * 4 + who) * ROWS + h) * 2 * chunk, 16), 2 * chunk)

    def send_out(a, row=None):
        stage, out = outs[a]
        count = ROWS if row is None else 1

        def which(i):
            return (i + zlo) % ROWS if row is None else row

        @pl.loop(0, count)
        def _(i):
            h = which(i)
            first = pl.multiple_of(h * tile + 2 * zlo * chunk, 16)
            pltpu.make_async_remote_copy(
                stage.at[pl.ds(first, 2 * chunk)], relay_buf.at[slot(a, x, h)], out_send.at[a],
                relay_recv.at[a, x, h], device_id=relay_dev, device_id_type=MESH,
            ).start()

        @pl.loop(0, 6 * count)
        def _(i):
            h, piece = which(i // 6), (2 * zlo + 2 + i % 6) % 8
            first = pl.multiple_of(h * tile + piece * chunk, 16)
            me = (core == zhi) & (zlo == h) & (piece == ten)

            @pl.when(me)
            def _():
                pltpu.make_async_copy(stage.at[pl.ds(first, chunk)], out.at[:, columns(head)], out_recv.at[a]).start()

            @pl.when(jnp.logical_not(me))
            def _():
                pltpu.make_async_remote_copy(
                    stage.at[pl.ds(first, chunk)], out.at[:, columns(head)], out_send.at[a], out_recv.at[a],
                    device_id=(frame, h, piece), device_id_type=MESH,
                ).start()

    def pass_on(a):
        _, out = outs[a]

        @pl.loop(0, 12)
        def _(i):
            h, who = (i // 3 + (zlo if a > 1 else 0)) % ROWS, (x + 1 + i % 3) % 4
            wait_bytes(relay_buf.at[slot(a, who, h)], relay_recv.at[a, who, h])
            base = pl.multiple_of(((a * 4 + who) * ROWS + h) * 2 * chunk, 16)
            cols = columns(head_of(who, z))
            for s in range(2):
                src = relay_buf.at[pl.ds(base + s * chunk, chunk)]
                me = (core == zhi) & (h == zlo) & (core == s)

                @pl.when(me)
                def _(src=src):
                    pltpu.make_async_copy(src, out.at[:, cols], out_recv.at[a]).start()

                @pl.when(jnp.logical_not(me))
                def _(src=src, s=s):
                    pltpu.make_async_remote_copy(
                        src, out.at[:, cols], out_send.at[a], out_recv.at[a],
                        device_id=(frame, h, 2 * x + s), device_id_type=MESH,
                    ).start()

    def forward(a, buf, d):
        piece = (x - d + 4) % 4 * 2 * chunk
        for side, has, dev in sides:
            @pl.when(has)
            def _(side=side, dev=dev):
                there = 2 - 2 * side
                for h in range(ROWS):
                    pltpu.make_async_remote_copy(
                        buf.at[pl.ds(pl.multiple_of((4 + h) * tile + piece, 16), 2 * chunk)],
                        buf.at[pl.ds(pl.multiple_of((4 * there + h) * tile + piece, 16), 2 * chunk)],
                        halo_send.at[side, a], halo_recv.at[1 - side, a], device_id=dev, device_id_type=MESH,
                    ).start()

    def arrived(a, d):
        wait_bytes(qb.at[rows(0)], in_recv.at[a, d])

    def halo_arrived(a, buf):
        for side, has, _ in sides:
            @pl.when(has)
            def _(side=side):
                wait_bytes(buf.at[rows(8 * side, 4)], halo_recv.at[side, a])

    def give_back(a, ret, got, r):
        for side, has, dev in sides:
            @pl.when(has)
            def _(side=side, dev=dev):
                pltpu.make_async_remote_copy(
                    ret.at[rows(4 * side + r)], got.at[rows(4 * (1 - side) + r)],
                    ret_send.at[side, a], ret_recv.at[1 - side, a, r], device_id=dev, device_id_type=MESH,
                ).start()

    def near_rows(h):
        lo, hi = max(h - 1, 0), min(h + 1, ROWS - 1)
        return lo, hi - lo + 1

    def pairs(h):
        lo, count = near_rows(h)
        return [(f, r) for f in range(3) for r in range(lo, lo + count)]

    def lanes(h, count=1):
        return pl.ds(h * tile, count * tile)

    def seen(h, f, r):
        reach_t, reach_h = ext_ref[h, 0, 0, frame], ext_ref[h, 1, 0, frame]
        inside = (f + frame >= 1) & (f + frame <= FRAMES)
        return inside & (abs(f - 1) <= reach_t) & (abs(r - h) <= reach_h)

    def over_rows(a, fn):
        return fn(a.reshape(tile // 8, 8, tile), axis=0)

    @pl.when(worker)
    def _():
        for side, has, _ in sides:
            @pl.when(jnp.logical_not(has))
            def _(side=side):
                for ref in (kb, vb):
                    ref[rows(8 * side, 4), :] = jnp.zeros((4 * tile, HD), BF)

        for d in range(4):
            arrived(K, d)
            forward(0, kb, d)
        for d in range(4):
            arrived(Q, d)
        for h in range(ROWS):
            qt[:, lanes(h)] = qb[rows(h), :].T
        halo_arrived(0, kb)

        inverse = []
        for h in range(ROWS):
            top = jnp.full((8, tile), LOW, F32)
            for f, r in pairs(h):
                s = dot(kb[rows(4 * f + r), :], qt[:, lanes(h)])
                s_all[rows(4 * f + r), :] = s
                top = jnp.maximum(top, jnp.where(seen(h, f, r), over_rows(s, jnp.max), LOW))
            top = jnp.max(top, axis=0, keepdims=True)
            total = jnp.zeros((8, tile), F32)
            for f, r in pairs(h):
                e = jnp.exp2((s_all[rows(4 * f + r), :] - jnp.where(seen(h, f, r), top, HIGH)) * c2)
                e_all[rows(4 * f + r), lanes(h)] = e.astype(BF)
                total = total + over_rows(e, jnp.sum)
            inverse.append(1.0 / jnp.sum(total, axis=0, keepdims=True))

        for d in range(4):
            arrived(V, d)
            forward(1, vb, d)

        def turn(to, buf, f):
            for h in range(ROWS):
                r = rows(4 * f + h)
                to[:, r] = buf[r, :].T

        turn(vt, vb, 1)
        for f in range(3):
            turn(kt, kb, f)
        halo_arrived(1, vb)
        turn(vt, vb, 0)
        turn(vt, vb, 2)

        def across(left, right, h):
            lo, count = near_rows(h)
            return sum(
                dot(left[:, rows(4 * f + lo, count)], right[rows(4 * f + lo, count), lanes(h)]) for f in range(3)
            )

        atts = []
        for h in range(ROWS):
            att = (across(vt, e_all, h) * inverse[h]).astype(BF)
            atts.append(att)
            att_s[rows(h), :] = att.T
            send_out(0, h)

        dots = []
        for d in range(4):
            arrived(G, d)
        for h in range(ROWS):
            g = (gb[rows(h), :].T.astype(F32) * inverse[h]).astype(BF)
            gt[:, lanes(h)] = g
            gn[rows(h), :] = g.T
            dots.append(jnp.sum(g.astype(F32) * atts[h].astype(F32), axis=0, keepdims=True))

        def key_term(left, right, f, r):
            lo, count = near_rows(r)
            return dot(left[rows(4 * f + r), lanes(lo, count)], right[rows(lo, count), :])

        for r in range(ROWS):
            for side in range(2):
                dv_ret[rows(4 * side + r), :] = key_term(e_all, gn, 2 * side, r).astype(BF)
            give_back(1, dv_ret, dv_got, r)
        for h in range(ROWS):
            for f, r in pairs(h):
                dp = dot(vb[rows(4 * f + r), :], gt[:, lanes(h)])
                e = e_all[rows(4 * f + r), lanes(h)].astype(F32)
                ds_all[rows(4 * f + r), lanes(h)] = (e * (dp - dots[h])).astype(BF)
            dq_s[rows(h), :] = (across(kt, ds_all, h) * scale).astype(BF).T
            send_out(1, h)

        for r in range(ROWS):
            for side in range(2):
                dk_ret[rows(4 * side + r), :] = (key_term(ds_all, qb, 2 * side, r) * scale).astype(BF)
            give_back(0, dk_ret, dk_got, r)

        def returned(a, got, r):
            for side, has, _ in sides:
                @pl.when(has)
                def _(side=side):
                    wait_bytes(got.at[rows(4 * side + r)], ret_recv.at[side, a, r])
            return [
                jnp.where(has, got[rows(4 * side + r), :].astype(F32), 0.0) for side, has, _ in sides
            ]

        for r in range(ROWS):
            a, b = returned(1, dv_got, r)
            dv_s[rows(r), :] = (key_term(e_all, gn, 1, r) + a + b).astype(BF)
        send_out(3)
        for r in range(ROWS):
            own = key_term(ds_all, qb, 1, r) * scale
            a, b = returned(0, dk_got, r)
            dk_s[rows(r), :] = (own + a + b).astype(BF)
        send_out(2)

        for side, has, _ in sides:
            @pl.when(has)
            def _(side=side):
                for a in range(2):
                    wait_bytes(kb.at[rows(0, 4)], halo_send.at[side, a])
                    wait_bytes(dk_ret.at[rows(0, 4)], ret_send.at[side, a])

        for a in range(4):
            @pl.when(core == zhi)
            def _(a=a):
                wait_bytes(att_s.at[pl.ds(0, 31 * chunk)], out_send.at[a])

            @pl.when(core != zhi)
            def _(a=a):
                wait_bytes(att_s, out_send.at[a])

    @pl.when(jnp.logical_not(worker))
    def _():
        for a in (0, 1, 3, 2):
            pass_on(a)
        for a in range(4):
            @pl.when(core == zhi)
            def _(a=a):
                wait_bytes(relay_buf.at[pl.ds(0, 21 * chunk)], out_send.at[a])

            @pl.when(core != zhi)
            def _(a=a):
                wait_bytes(relay_buf.at[pl.ds(0, 24 * chunk)], out_send.at[a])

    for a in range(4):
        @pl.when(mine)
        def _(a=a):
            wait_bytes(q_ref.at[:, pl.ds(0, 23 * HD)], in_send.at[a])

        @pl.when(jnp.logical_not(mine))
        def _(a=a):
            wait_bytes(q_ref, in_send.at[a])

    for a, (_, out) in enumerate(outs):
        wait_bytes(out, out_recv.at[a])


def settle(*refs):
    froms, tos, held, loaded, stored = refs[:4], refs[4:8], refs[8:12], refs[12], refs[13]
    loads = [pltpu.make_async_copy(a, b, loaded.at[i]) for i, (a, b) in enumerate(zip(froms, held))]
    stores = [pltpu.make_async_copy(a, b, stored.at[i]) for i, (a, b) in enumerate(zip(held, tos))]
    for load in loads:
        load.start()
    for load, store in zip(loads, stores):
        load.wait()
        store.start()
    for store in stores:
        store.wait()


def solution(mesh):
    spec = P("tm", "height", None, "tensor", None)

    def shards(query, keys, values, cotangent, extents):
        shape = query.shape
        chunk, width = shape[3], shape[4]
        tile = chunk * mesh.shape["tensor"]
        flat = [a.reshape(chunk, width) for a in (query, keys, values, cotangent)]
        any_spec = pl.BlockSpec(memory_space=pl.ANY)
        four = ROWS * tile
        dma = pltpu.SemaphoreType.DMA
        pieces = [jax.ShapeDtypeStruct((chunk, width), BF)] * 4
        outs = pl.pallas_call(
            functools.partial(kernel, tile, chunk),
            out_shape=pieces,
            in_specs=[pl.BlockSpec(memory_space=pltpu.SMEM)] + [any_spec] * 4,
            out_specs=[any_spec] * 4,
            scratch_shapes=[
                *[pltpu.VMEM((four, HD), BF)] * 2,
                *[pltpu.VMEM((3 * four, HD), BF)] * 2,
                *[pltpu.VMEM((HD, 3 * four), BF)] * 2,
                *[pltpu.VMEM((HD, four), BF)] * 2,
                pltpu.VMEM((four, HD), BF),
                pltpu.VMEM((3 * four, tile), F32),
                *[pltpu.VMEM((3 * four, four), BF)] * 2,
                *[pltpu.VMEM((four, HD), BF)] * 4,
                *[pltpu.VMEM((2 * four, HD), BF)] * 4,
                pltpu.VMEM((4 * 4 * ROWS * 2 * chunk, HD), BF),
                dma((4,)), dma((4, 4)), dma((2, 2)), dma((2, 2)),
                dma((2, 2)), dma((2, 2, 4)), dma((4,)), dma((4,)), dma((4, 4, ROWS)),
            ],
            compiler_params=pltpu.CompilerParams(
                collective_id=0, has_side_effects=True, vmem_limit_bytes=58 * 2**20
            ),
            name="attention",
        )(jnp.transpose(extents, (1, 3, 2, 0)), *flat)
        outs = pl.pallas_call(
            settle,
            out_shape=pieces,
            in_specs=[any_spec] * 4,
            out_specs=[any_spec] * 4,
            scratch_shapes=[*[pltpu.VMEM((chunk, width), BF)] * 4, dma((4,)), dma((4,))],
            compiler_params=pltpu.CompilerParams(vmem_limit_bytes=58 * 2**20),
            name="settle",
        )(*outs)
        return tuple(o.reshape(shape) for o in outs)

    return jax.shard_map(
        shards, mesh=mesh, in_specs=(spec, spec, spec, spec, P()), out_specs=(spec,) * 4, check_vma=False
    )
```
